32 devices in a mesh: group: 4 (over z), local: 4 (over y, x), rep: 2 (over core).
Axes of the slice: x: 2, y: 2, z: 4, core: 2. Of those that a mesh axis runs over, the one named last changes fastest.
Arguments:
- tokens: bfloat16 [2048, 2560], P(('rep', 'group', 'local')), parts along dimension 0, may hold values from -6 to 6
- gates: bfloat16 [2048, 8], P(('rep', 'group', 'local')), parts along dimension 0, may hold values from 0.049804688 to 1
- expert_ids: int32 [2048, 8], P(('rep', 'group', 'local')), parts along dimension 0, may hold values from 0 to 15, as said below
- w_gate: bfloat16 [16, 2560, 768], P(('group', 'local')), may hold values from -0.125 to 0.125
- w_up: bfloat16 [16, 2560, 768], P(('group', 'local')), may hold values from -0.125 to 0.125
- w_down: bfloat16 [16, 768, 2560], P(('group', 'local')), may hold values from -0.21875 to 0.21875
Outputs:
- mixed: bfloat16 [2048, 2560], P(('rep', 'group', 'local')), parts along dimension 0
The draws below stay inside these ranges and needn't reach their ends.
There are 2 independent parts, one for each index of `rep`. The reference program is written for one: setup_inputs(seed, part) draws one part's arguments, and reference() takes and returns one part's arrays. A program takes and returns all parts, laid end to end along the dimension named above; an argument that names none is the same for every part. Nothing has to cross between parts.
Inputs may be any that keep to these rules, and one draw needn't show every extreme that they name: `expert_ids`: each row names 8 different experts, which lie in at most 4 groups (expert // 4).
All inputs are finite; a program needn't handle non-finite values.
Results may differ from the reference program's by a relative error of at most 0.0057.
Values may be sent and summed in bfloat16 or wider, within the bound.
No kernel may reach another device: no remote copies, remote signals or barrier semaphores. Data moves between devices by JAX's collectives and lax.ppermute only.
A program may use at most 64 MiB of HBM per device.

```python
import math
import jax
import jax.numpy as jnp
from jax import lax

D = 2560
FF = 768
TOP = 8
GROUPS_TOK = 4
TOK_DEV = 64
GROUPS = 4
EXP_GROUP = 4
EXPERTS = 16
TOKENS = 1024
PAIR_CAP = 64


def draw_expert_ids(key, part):
    key_hot, key_group, key_ehot, key_expert = jax.random.split(key, 4)
    group_hot = jax.random.randint(key_hot, (GROUPS,), 0, 3000)
    group_affinity = jax.random.randint(key_group, (TOKENS, GROUPS), 0, 4000) + group_hot
    group_affinity = group_affinity * 128 + jnp.arange(GROUPS, dtype=jnp.int32)
    _, picked_groups = lax.top_k(group_affinity, GROUPS_TOK)
    candidate_experts = (picked_groups[:, :, None] * EXP_GROUP + jnp.arange(EXP_GROUP, dtype=jnp.int32)).reshape(TOKENS, GROUPS_TOK * EXP_GROUP)
    expert_hot = jax.random.randint(key_ehot, (EXPERTS,), 0, 3000)
    expert_affinity = jax.random.randint(key_expert, (TOKENS, GROUPS_TOK * EXP_GROUP), 0, 4000) + expert_hot[candidate_experts]
    expert_affinity = expert_affinity * 256 + jnp.arange(GROUPS_TOK * EXP_GROUP, dtype=jnp.int32)
    _, picks = lax.top_k(expert_affinity, TOP)
    return jnp.take_along_axis(candidate_experts, picks, axis=1).astype(jnp.int32)


def level_of(key, dims, pieces, low, largest):
    def one(axis_at, parts):
        steps = jax.random.uniform(jax.random.fold_in(jax.random.fold_in(key, 6), axis_at), (parts,), jnp.float32, low / len(pieces), largest / len(pieces))
        return jnp.repeat(jnp.exp(steps), dims[axis_at] // parts).reshape((-1,) + (1,) * (len(dims) - axis_at - 1))

    gain = one(*pieces[0])
    for cut in pieces[1:]:
        gain = gain * one(*cut)
    return gain


def scatter_about(stream_key, shape, deviation, reach, cuts=(), kind=jnp.bfloat16):
    factor_of = level_of(stream_key, shape, cuts, -0.22, 0.18) if cuts else 1.0
    drawn = jax.random.normal(stream_key, shape, jnp.float32) * deviation * factor_of
    return jnp.minimum(jnp.maximum(drawn, -reach), reach).astype(kind)


def setup_inputs(seed: int = 0, part: int = 0) -> dict:
    arg_keys = jax.random.split(jax.random.key(seed), 7)
    part_splits = jax.random.split(jax.random.fold_in(arg_keys[6], part), 7)
    tokens = scatter_about(part_splits[0], (TOKENS, D), 1.0, 6.0, ((0, 16),))
    gates = jnp.clip(jnp.exp(math.log(1.0) - 2.9996462 * jax.random.uniform(part_splits[1], (TOKENS, TOP), jnp.float32) ** level_of(part_splits[1], (TOKENS, TOP), ((0, 16),), -0.2, 0.2)), 0.049804688, 1.0).astype(jnp.bfloat16)
    expert_ids = draw_expert_ids(jax.random.fold_in(jax.random.fold_in(arg_keys[6], part), 71), part)
    w_gate = scatter_about(arg_keys[3], (EXPERTS, D, FF), D ** -0.5, 0.125, ((0, 16),))
    w_up = scatter_about(arg_keys[4], (EXPERTS, D, FF), D ** -0.5, 0.125, ((0, 16),))
    w_down = scatter_about(arg_keys[5], (EXPERTS, FF, D), FF ** -0.5, 0.21875, ((0, 16),))
    return dict(tokens=tokens, gates=gates, expert_ids=expert_ids, w_gate=w_gate, w_up=w_up, w_down=w_down)


def expert_rows(rows, gate_mat, up_mat, down_mat):
    gate = jnp.dot(rows, gate_mat, preferred_element_type=jnp.float32)
    up = jnp.dot(rows, up_mat, preferred_element_type=jnp.float32)
    hidden = (jax.nn.silu(gate) * up).astype(jnp.bfloat16)
    return jnp.dot(hidden, down_mat, preferred_element_type=jnp.float32).astype(jnp.bfloat16)


def reference(tokens, gates, expert_ids, w_gate, w_up, w_down):
    blocks = GROUPS * EXP_GROUP
    input_rows = tokens.reshape(blocks, TOK_DEV, D)
    chosen = expert_ids.reshape(blocks, TOK_DEV, TOP)
    gate_vals = gates.reshape(blocks, TOK_DEV, TOP).astype(jnp.float32)
    expert_iota = jnp.arange(EXPERTS, dtype=jnp.int32)
    hits = chosen[..., None] == expert_iota
    weights = jnp.sum(jnp.where(hits, gate_vals[..., None], jnp.float32(0.0)), axis=2)
    member = jnp.any(jnp.any(hits, axis=2).reshape(blocks, TOK_DEV, GROUPS, EXP_GROUP), axis=3).astype(jnp.int32)
    rank = jnp.cumsum(member, axis=1) - member
    slot_iota = jnp.arange(PAIR_CAP, dtype=jnp.int32)
    place = ((member[..., None] == 1) & (rank[..., None] == slot_iota)).astype(jnp.float32)
    dispatched = jnp.einsum("stgc,std->sgcd", place, input_rows.astype(jnp.float32)).astype(jnp.bfloat16)
    slot_weights = jnp.einsum("stgc,stgl->sgcl", place, weights.reshape(blocks, TOK_DEV, GROUPS, EXP_GROUP), precision=lax.Precision.HIGHEST)

    def step(total, expert):
        group_idx = (expert // EXP_GROUP).astype(jnp.int32)
        local_idx = (expert % EXP_GROUP).astype(jnp.int32)
        rows = lax.dynamic_index_in_dim(dispatched, group_idx, 1, keepdims=False).reshape(blocks * PAIR_CAP, D)
        outputs = expert_rows(rows, lax.dynamic_index_in_dim(w_gate, expert, 0, keepdims=False), lax.dynamic_index_in_dim(w_up, expert, 0, keepdims=False), lax.dynamic_index_in_dim(w_down, expert, 0, keepdims=False))
        group_w = lax.dynamic_index_in_dim(slot_weights, group_idx, 1, keepdims=False)
        expert_w = lax.dynamic_index_in_dim(group_w, local_idx, 2, keepdims=False)
        terms = expert_w[..., None] * outputs.reshape(blocks, PAIR_CAP, D).astype(jnp.float32)
        group_place = lax.dynamic_index_in_dim(place, group_idx, 2, keepdims=False)
        total = total + jnp.einsum("stc,scd->std", group_place, terms, precision=lax.Precision.HIGHEST)
        return total, None

    start = jnp.zeros((blocks, TOK_DEV, D), jnp.float32)
    total, _ = lax.scan(step, start, jnp.arange(EXPERTS, dtype=jnp.int32))
    return total.reshape(TOKENS, D).astype(jnp.bfloat16)
```

```python
import functools

import jax
import jax.numpy as jnp
from jax import lax
from jax.experimental import pallas as pl
from jax.experimental.pallas import tpu as pltpu
from jax.sharding import PartitionSpec as P

GROUPS_TOK = 4
VMEM_LIMIT = 60 * 2**20


def expert_rows(rows, gate_mat, up_mat, down_mat):
    gate = jnp.dot(rows, gate_mat, preferred_element_type=jnp.float32)
    up = jnp.dot(rows, up_mat, preferred_element_type=jnp.float32)
    hidden = (jax.nn.silu(gate) * up).astype(jnp.bfloat16)
    return jnp.dot(hidden, down_mat, preferred_element_type=jnp.float32).astype(jnp.bfloat16)


def routed_shards(tokens, gates, expert_ids, w_gate, w_up, w_down):
    tok_rows, width = tokens.shape
    n_group = lax.axis_size("group")
    local_expert_count = lax.axis_size("local")
    capacity = min(tok_rows, tok_rows * GROUPS_TOK // n_group)
    expert_iota = jnp.arange(n_group * local_expert_count, dtype=jnp.int32)
    hits = expert_ids[:, :, None] == expert_iota
    weights = jnp.sum(
        jnp.where(hits, gates.astype(jnp.float32)[:, :, None], jnp.float32(0.0)), axis=1
    )
    member = jnp.any(
        jnp.any(hits, axis=1).reshape(tok_rows, n_group, local_expert_count), axis=2
    ).astype(jnp.int32)
    rank = jnp.cumsum(member, axis=0) - member
    slot_iota = jnp.arange(capacity, dtype=jnp.int32)
    place = (member[:, :, None] == 1) & (rank[:, :, None] == slot_iota)
    place_f = place.astype(jnp.float32)
    outgoing = jnp.einsum(
        "tgc,td->gcd", place.astype(jnp.bfloat16), tokens, preferred_element_type=jnp.float32
    ).astype(jnp.bfloat16)
    slot_weights = jnp.einsum(
        "tgc,tgl->gcl",
        place_f,
        weights.reshape(tok_rows, n_group, local_expert_count),
        precision=lax.Precision.HIGHEST,
    ).astype(jnp.bfloat16)
    send_rows = jnp.broadcast_to(
        outgoing[:, None], (n_group, local_expert_count, capacity, width)
    ).reshape(n_group * local_expert_count, capacity, width)
    send_weights = jnp.transpose(slot_weights, (0, 2, 1)).reshape(
        n_group * local_expert_count, capacity
    )
    received_rows, got_weights = (
        lax.all_to_all(send_rows, ("group", "local"), split_axis=0, concat_axis=0, tiled=True),
        lax.all_to_all(send_weights, ("group", "local"), split_axis=0, concat_axis=0, tiled=True),
    )
    arrived = received_rows.reshape(n_group, local_expert_count, capacity, width)
    own_weights = got_weights.reshape(n_group, local_expert_count, capacity)
    outputs = expert_rows(
        arrived.reshape(n_group * local_expert_count * capacity, width),
        w_gate[0],
        w_up[0],
        w_down[0],
    )
    outputs = outputs.reshape(n_group, local_expert_count, capacity, width)
    masked = jnp.where(own_weights[..., None] > 0, outputs, jnp.zeros_like(outputs))
    returned_rows = lax.all_to_all(
        masked.reshape(n_group * local_expert_count, capacity, width),
        ("group", "local"),
        split_axis=0,
        concat_axis=0,
        tiled=True,
    )
    returned_rows = returned_rows.reshape(n_group, local_expert_count, capacity, width)
    sender_weights = jnp.transpose(slot_weights, (0, 2, 1))
    combined = jnp.einsum(
        "zqa,zqap->zap", sender_weights, returned_rows, preferred_element_type=jnp.float32
    )
    mixed = jnp.einsum("tgc,gcd->td", place_f, combined, precision=lax.Precision.HIGHEST)
    return mixed.astype(jnp.bfloat16)


def over(axis, mask):
    pairs = [(i, i ^ mask) for i in range(4)]
    return lambda v: lax.ppermute(v, axis, pairs)


def expert_kernel(n_pieces, ff_tile, out_tile, me_ref, *refs):
    pieces = refs[:n_pieces]
    wg_hbm, wu_hbm, wd_hbm = refs[n_pieces : n_pieces + 3]
    outs = refs[n_pieces + 3 : n_pieces + 7]
    rows, wg, wu, wd, hidden, send, keep, sems = refs[n_pieces + 7 :]
    ff, width = wd.shape
    n_ff, n_out = ff // ff_tile, width // out_tile
    n_rows = rows.shape[0]
    block = n_rows // 8

    row_copies, at = [], 0
    for piece in pieces:
        size = piece.shape[0]
        row_copies.append((piece, rows.at[pl.ds(at, size)]))
        at += size
    ff_copies = []
    for f in range(n_ff):
        cols = pl.ds(f * ff_tile, ff_tile)
        ff_copies.append((wg_hbm.at[0, :, cols], wg.at[f]))
        ff_copies.append((wu_hbm.at[0, :, cols], wu.at[f]))
    down_copies = [(wd_hbm.at[0], wd)]
    loads = [
        pltpu.make_async_copy(src, dst, sems.at[i])
        for i, (src, dst) in enumerate(ff_copies[:2] + row_copies + ff_copies[2:] + down_copies)
    ]
    for load in loads:
        load.start()

    head = 2 + n_pieces
    for load in loads[:head]:
        load.wait()
    table = rows[:, pl.ds(width, 128)].astype(jnp.float32)
    lane = lax.broadcasted_iota(jnp.int32, table.shape, 1)
    scale = jnp.sum(jnp.where(lane == me_ref[0], table, 0.0), axis=1, keepdims=True)
    for f in range(n_ff):
        if f:
            loads[head + 2 * f - 2].wait()
            loads[head + 2 * f - 1].wait()
        x = rows[:, pl.ds(0, width)]
        gate = jnp.dot(x, wg[f], preferred_element_type=jnp.float32)
        up = jnp.dot(x, wu[f], preferred_element_type=jnp.float32)
        hidden[:, pl.ds(f * ff_tile, ff_tile)] = (jax.nn.silu(gate) * up).astype(jnp.bfloat16)
    for load in loads[head + 2 * n_ff - 2 :]:
        load.wait()
    stores = []
    for n in range(n_out):
        cols = pl.ds(n * out_tile, out_tile)
        out = jnp.dot(hidden[...], wd[:, cols], preferred_element_type=jnp.float32) * scale
        for stage in range(2):
            at = 4 * stage * block
            keep[stage, :, cols] = out[at : at + 2 * block]
            send[stage, :, cols] = out[at + 2 * block : at + 4 * block].astype(jnp.bfloat16)
            for src, dst in ((send, outs[stage]), (keep, outs[2 + stage])):
                store = pltpu.make_async_copy(
                    src.at[stage, :, cols], dst.at[:, cols], sems.at[len(loads) + len(stores)]
                )
                store.start()
                stores.append(store)
    for store in stores:
        store.wait()


def experts(first, second, me, w_gate, w_up, w_down):
    pieces = [*first, *second]
    n_rows = sum(p.shape[0] for p in pieces)
    wide = pieces[0].shape[1]
    _, width, ff = w_gate.shape
    ff_tile, out_tile = ff // 3, width // 5
    half = n_rows // 4
    n_sems = len(pieces) + 7 + 4 * (width // out_tile)
    hbm = pl.BlockSpec(memory_space=pltpu.HBM)
    return pl.pallas_call(
        functools.partial(expert_kernel, len(pieces), ff_tile, out_tile),
        out_shape=[
            jax.ShapeDtypeStruct((half, width), jnp.bfloat16),
            jax.ShapeDtypeStruct((half, width), jnp.bfloat16),
            jax.ShapeDtypeStruct((half, width), jnp.float32),
            jax.ShapeDtypeStruct((half, width), jnp.float32),
        ],
        in_specs=[
            pl.BlockSpec(memory_space=pltpu.SMEM),
            *([hbm] * (len(pieces) + 3)),
        ],
        out_specs=[hbm] * 4,
        scratch_shapes=[
            pltpu.VMEM((n_rows, wide), jnp.bfloat16),
            pltpu.VMEM((3, width, ff_tile), jnp.bfloat16),
            pltpu.VMEM((3, width, ff_tile), jnp.bfloat16),
            pltpu.VMEM((ff, width), jnp.bfloat16),
            pltpu.VMEM((n_rows, ff), jnp.bfloat16),
            pltpu.VMEM((2, half, width), jnp.bfloat16),
            pltpu.VMEM((2, half, width), jnp.float32),
            pltpu.SemaphoreType.DMA((n_sems,)),
        ],
        compiler_params=pltpu.CompilerParams(vmem_limit_bytes=VMEM_LIMIT),
        cost_estimate=pl.CostEstimate(
            flops=6 * n_rows * width * ff,
            bytes_accessed=6 * width * ff + 5 * n_rows * width,
            transcendentals=n_rows * ff,
        ),
    )(me, *pieces, w_gate, w_up, w_down)


def after(value, *done):
    return lax.optimization_barrier((value, *done))[0]


def gathered_shards(tokens, gates, expert_ids, w_gate, w_up, w_down):
    block = tokens.shape[0]
    X, Y = over("local", 1), over("local", 2)
    Z1, Z2 = over("group", 1), over("group", 2)
    me = lax.axis_index("group") * 4 + lax.axis_index("local")

    lanes = jnp.arange(128, dtype=jnp.int32)
    hits = expert_ids[:, :, None] == lanes
    weights = jnp.sum(jnp.where(hits, gates[:, :, None], jnp.bfloat16(0.0)), axis=1)
    own = jnp.concatenate([tokens, weights], axis=1)

    e1, e2 = Z1(own), Z2(own)
    own_x, own_y = X(own), Y(own)
    own_d = Y(own_x)
    e3 = Z1(e2)
    e2_x, e2_y = X(after(e2, own_x)), Y(after(e2, own_y))
    e2_d = Y(e2_x)
    e3_y, e3_x = Y(after(e3, e2_y)), X(after(e3, e2_x))
    e3_d = X(e3_y)
    e1_ = after(e1, e3_x, e2_d)
    e1_y, e1_x = Y(e1_), X(e1_)
    e1_d = X(e1_y)

    me = me.astype(jnp.int32).reshape(1)
    far = experts((e2, e2_x, e2_y, e2_d), (e3, e3_y, e3_x, e3_d), me, w_gate, w_up, w_down)
    near = experts((own, own_x, own_y, own_d), (after(e1, far[0]), e1_y, e1_x, e1_d), me, w_gate, w_up, w_down)

    f32 = jnp.float32

    def summed(outs):
        send_p, send_q, keep_p, keep_q = outs
        got_p, got_q = Y(send_p), X(send_q)
        last_p = X((keep_p[block:] + got_p[block:].astype(f32)).astype(jnp.bfloat16))
        last_q = Y((keep_q[block:] + got_q[block:].astype(f32)).astype(jnp.bfloat16))
        return (
            keep_p[:block] + got_p[:block].astype(f32) + last_p.astype(f32),
            keep_q[:block] + got_q[:block].astype(f32) + last_q.astype(f32),
        )

    r2, r3 = summed(far)
    r2 = r2 + Z1(r3.astype(jnp.bfloat16)).astype(f32)
    b2 = Z2(r2.astype(jnp.bfloat16))
    r0, r1 = summed(near)
    b1 = Z1(r1.astype(jnp.bfloat16))
    return (r0 + b1.astype(f32) + b2.astype(f32)).astype(jnp.bfloat16)


def shards(tokens, *rest):
    tok_rows = tokens.shape[0]
    n_group, n_local = lax.axis_size("group"), lax.axis_size("local")
    capacity = min(tok_rows, tok_rows * GROUPS_TOK // n_group)
    if capacity == tok_rows and n_group == 4 and n_local == 4:
        return gathered_shards(tokens, *rest)
    return routed_shards(tokens, *rest)


def solution(mesh):
    in_specs = (
        P(("rep", "group", "local"), None),
        P(("rep", "group", "local"), None),
        P(("rep", "group", "local"), None),
        P(("group", "local"), None, None),
        P(("group", "local"), None, None),
        P(("group", "local"), None, None),
    )
    out_specs = P(("rep", "group", "local"), None)
    return jax.shard_map(shards, mesh=mesh, in_specs=in_specs, out_specs=out_specs, check_vma=False)
```

```python
import functools

import jax
import jax.numpy as jnp
from jax import lax
from jax.experimental import pallas as pl
from jax.experimental.pallas import tpu as pltpu
from jax.sharding import PartitionSpec as P

GROUPS_TOK = 4
VMEM_LIMIT = 16 * 2**20


def expert_rows(rows, gate_mat, up_mat, down_mat):
    gate = jnp.dot(rows, gate_mat, preferred_element_type=jnp.float32)
    up = jnp.dot(rows, up_mat, preferred_element_type=jnp.float32)
    hidden = (jax.nn.silu(gate) * up).astype(jnp.bfloat16)
    return jnp.dot(hidden, down_mat, preferred_element_type=jnp.float32).astype(jnp.bfloat16)


def routed_shards(tokens, gates, expert_ids, w_gate, w_up, w_down):
    tok_rows, width = tokens.shape
    n_group = lax.axis_size("group")
    local_expert_count = lax.axis_size("local")
    capacity = min(tok_rows, tok_rows * GROUPS_TOK // n_group)
    expert_iota = jnp.arange(n_group * local_expert_count, dtype=jnp.int32)
    hits = expert_ids[:, :, None] == expert_iota
    weights = jnp.sum(
        jnp.where(hits, gates.astype(jnp.float32)[:, :, None], jnp.float32(0.0)), axis=1
    )
    member = jnp.any(
        jnp.any(hits, axis=1).reshape(tok_rows, n_group, local_expert_count), axis=2
    ).astype(jnp.int32)
    rank = jnp.cumsum(member, axis=0) - member
    slot_iota = jnp.arange(capacity, dtype=jnp.int32)
    place = (member[:, :, None] == 1) & (rank[:, :, None] == slot_iota)
    place_f = place.astype(jnp.float32)
    outgoing = jnp.einsum(
        "tgc,td->gcd", place.astype(jnp.bfloat16), tokens, preferred_element_type=jnp.float32
    ).astype(jnp.bfloat16)
    slot_weights = jnp.einsum(
        "tgc,tgl->gcl",
        place_f,
        weights.reshape(tok_rows, n_group, local_expert_count),
        precision=lax.Precision.HIGHEST,
    ).astype(jnp.bfloat16)
    send_rows = jnp.broadcast_to(
        outgoing[:, None], (n_group, local_expert_count, capacity, width)
    ).reshape(n_group * local_expert_count, capacity, width)
    send_weights = jnp.transpose(slot_weights, (0, 2, 1)).reshape(
        n_group * local_expert_count, capacity
    )
    received_rows, got_weights = (
        lax.all_to_all(send_rows, ("group", "local"), split_axis=0, concat_axis=0, tiled=True),
        lax.all_to_all(send_weights, ("group", "local"), split_axis=0, concat_axis=0, tiled=True),
    )
    arrived = received_rows.reshape(n_group, local_expert_count, capacity, width)
    own_weights = got_weights.reshape(n_group, local_expert_count, capacity)
    outputs = expert_rows(
        arrived.reshape(n_group * local_expert_count * capacity, width),
        w_gate[0],
        w_up[0],
        w_down[0],
    )
    outputs = outputs.reshape(n_group, local_expert_count, capacity, width)
    masked = jnp.where(own_weights[..., None] > 0, outputs, jnp.zeros_like(outputs))
    returned_rows = lax.all_to_all(
        masked.reshape(n_group * local_expert_count, capacity, width),
        ("group", "local"),
        split_axis=0,
        concat_axis=0,
        tiled=True,
    )
    returned_rows = returned_rows.reshape(n_group, local_expert_count, capacity, width)
    sender_weights = jnp.transpose(slot_weights, (0, 2, 1))
    combined = jnp.einsum(
        "zqa,zqap->zap", sender_weights, returned_rows, preferred_element_type=jnp.float32
    )
    mixed = jnp.einsum("tgc,gcd->td", place_f, combined, precision=lax.Precision.HIGHEST)
    return mixed.astype(jnp.bfloat16)


def over(axis, mask):
    pairs = [(i, i ^ mask) for i in range(4)]
    return lambda v: lax.ppermute(v, axis, pairs)


def expert_kernel(n_pieces, ff_tile, out_tile, me_ref, *refs, loads=()):
    pieces = refs[:n_pieces]
    wg, wu, wd = refs[n_pieces : n_pieces + 3]
    *outs, hidden = refs[n_pieces + 3 :]
    _, ff, width = wd.shape

    table = jnp.concatenate([p[:, pl.ds(width, 128)] for p in pieces], axis=0).astype(jnp.float32)
    lane = lax.broadcasted_iota(jnp.int32, table.shape, 1)
    scale = jnp.sum(jnp.where(lane == me_ref[0], table, 0.0), axis=1, keepdims=True)
    for f in range(ff // ff_tile):
        cols = pl.ds(f * ff_tile, ff_tile)
        for load in loads[2 * f : 2 * f + 2]:
            load.wait()
        x = jnp.concatenate([p[:, pl.ds(0, width)] for p in pieces], axis=0)
        gate = jnp.dot(x, wg[0, :, cols], preferred_element_type=jnp.float32)
        up = jnp.dot(x, wu[0, :, cols], preferred_element_type=jnp.float32)
        hidden[:, cols] = (jax.nn.silu(gate) * up).astype(jnp.bfloat16)
    for load in loads[2 * (ff // ff_tile) :]:
        load.wait()
    for n in range(width // out_tile):
        cols = pl.ds(n * out_tile, out_tile)
        out = jnp.dot(hidden[...], wd[0, :, cols], preferred_element_type=jnp.float32) * scale
        at = 0
        for buf in outs:
            size = buf.shape[0]
            buf[:, cols] = out[at : at + size].astype(buf.dtype)
            at += size


def first_kernel(n_pieces, ff_tile, out_tile, me_ref, *refs):
    weights_hbm = refs[n_pieces : n_pieces + 3]
    weights = refs[n_pieces + 3 : n_pieces + 6]
    load_sems = refs[-1]
    ff = weights[0].shape[2]
    loads, pairs = [], []
    for f in range(ff // ff_tile):
        cols = pl.ds(f * ff_tile, ff_tile)
        pairs += [(w_hbm.at[0, :, cols], w.at[0, :, cols]) for w_hbm, w in zip(weights_hbm[:2], weights[:2])]
    pairs.append((weights_hbm[2], weights[2]))
    for i, (src, dst) in enumerate(pairs):
        loads.append(pltpu.make_async_copy(src, dst, load_sems.at[i]))
        loads[-1].start()
    expert_kernel(
        n_pieces, ff_tile, out_tile, me_ref, *refs[:n_pieces], *weights, *refs[n_pieces + 6 : -1], loads=loads
    )


def experts(pieces, outs, me, weights, first=False):
    n_rows = sum(p.shape[0] for p in pieces)
    _, width, ff = weights[0].shape
    ff_tile, out_tile = ff // 3, width // 5
    vmem = pl.BlockSpec(memory_space=pltpu.VMEM)
    if first:
        weights = [pltpu.with_memory_space_constraint(w, pltpu.HBM) for w in weights]
    return pl.pallas_call(
        functools.partial(first_kernel if first else expert_kernel, len(pieces), ff_tile, out_tile),
        out_shape=[
            *(pltpu.VMEM(w.shape, w.dtype) for w in weights if first),
            *(pltpu.VMEM((rows, width), dtype) for rows, dtype in outs),
        ],
        in_specs=[
            pl.BlockSpec(memory_space=pltpu.SMEM),
            *([vmem] * len(pieces)),
            *([pl.BlockSpec(memory_space=pltpu.HBM) if first else vmem] * 3),
        ],
        out_specs=[vmem] * (len(outs) + 3 * first),
        scratch_shapes=[
            pltpu.VMEM((n_rows, ff), jnp.bfloat16),
            *([pltpu.SemaphoreType.DMA((7,))] if first else []),
        ],
        compiler_params=pltpu.CompilerParams(vmem_limit_bytes=VMEM_LIMIT),
        cost_estimate=pl.CostEstimate(
            flops=6 * n_rows * width * ff,
            bytes_accessed=8 * n_rows * width,
            transcendentals=n_rows * ff,
        ),
    )(me, *pieces, *weights)


def after(value, *done):
    return lax.optimization_barrier((value, *done))[0]


def gathered_shards(tokens, gates, expert_ids, w_gate, w_up, w_down):
    block = tokens.shape[0]
    X, Y = over("local", 1), over("local", 2)
    Z1, Z2 = over("group", 1), over("group", 2)
    me = lax.axis_index("group") * 4 + lax.axis_index("local")

    lanes = jnp.arange(128, dtype=jnp.int32)
    hits = expert_ids[:, :, None] == lanes
    weights = jnp.sum(jnp.where(hits, gates[:, :, None], jnp.bfloat16(0.0)), axis=1)
    own = jnp.concatenate([tokens, weights], axis=1)

    half = block // 2
    f32, bf16 = jnp.float32, jnp.bfloat16
    me = me.astype(jnp.int32).reshape(1)

    e1, own_x, own_y, e2 = Z1(own), X(own), Y(own), Z2(own)
    own_a, own_b = Y(own_x[:half]), X(own_y[half:])
    *weights, k0, k0_x, k0_y = experts(
        (own, own_x, own_y), ((block, f32),) * 3, me, (w_gate, w_up, w_down), first=True
    )
    e1_y = Y(after(e1, own_a, own_b))
    e2_ = after(e2, own_a, own_b, e1, k0_x)
    e2_x, e2_y, e3 = X(e2_), Y(e2_), Z1(e2_)
    e3_ = after(e3)
    e3_x, e3_y = X(e3_), Y(e3_)
    e1_xd = Z1(after(jnp.concatenate([own_x, own_a, own_b]), e3))
    e2_d = X(after(e2_y, e2_x))
    k0_d, k1, send_1 = experts(
        (own_a, own_b, e1, e1_y), ((block, f32), (block, f32), (block, bf16)), me, weights
    )
    e3_x, e3_y = lax.optimization_barrier((e3_x, e3_y, k1))[:2]
    e3_a, e3_b = Y(e3_x[:half]), X(e3_y[half:])
    k2, k2_y, send_2 = experts(
        (e2, e2_y, e2_x, e2_d), ((block, f32), (block, f32), (2 * block, bf16)), me, weights
    )
    k3, k3_x, k3_y, send_a, send_b, to_own = experts(
        (after(e3, send_2), e3_x, e3_y, e3_a, e3_b, e1_xd),
        (*(((block, f32),) * 3), *(((half, bf16),) * 2), (2 * block, bf16)),
        me,
        weights,
    )

    def joined(part_x, part_y, got_a, got_b):
        part_x = jnp.concatenate([part_x[:half] + got_a.astype(f32), part_x[half:]])
        part_y = jnp.concatenate([part_y[:half], part_y[half:] + got_b.astype(f32)])
        return X(part_x.astype(bf16)), Y(part_y.astype(bf16))

    got_2 = X(send_2)
    got_a, got_b = Y(send_a), X(send_b)
    got_x, got_y = joined(k3_x, k3_y, got_a, got_b)
    r3 = (k3 + got_x.astype(f32) + got_y.astype(f32)).astype(bf16)
    last_2 = Y((k2_y + got_2[block:].astype(f32)).astype(bf16))
    r2 = k2 + got_2[:block].astype(f32) + last_2.astype(f32)
    r2 = r2 + Z1(r3).astype(f32)
    from_far = Z2(r2.astype(bf16))
    from_1 = Z1(to_own)
    r1 = k1 + Y(after(send_1, got_a, got_b)).astype(f32)
    from_near = Z1(r1.astype(bf16))
    k0_x = k0_x + from_1[:block].astype(f32)
    k0_d = (k0_d + from_1[block:].astype(f32)).astype(bf16)
    got_x, got_y = joined(k0_x, k0_y, Y(k0_d[:half]), X(k0_d[half:]))
    r0 = k0 + got_x.astype(f32) + got_y.astype(f32)
    return (r0 + from_near.astype(f32) + from_far.astype(f32)).astype(bf16)


def shards(tokens, *rest):
    tok_rows = tokens.shape[0]
    n_group, n_local = lax.axis_size("group"), lax.axis_size("local")
    capacity = min(tok_rows, tok_rows * GROUPS_TOK // n_group)
    if capacity == tok_rows and n_group == 4 and n_local == 4:
        return gathered_shards(tokens, *rest)
    return routed_shards(tokens, *rest)


def solution(mesh):
    in_specs = (
        P(("rep", "group", "local"), None),
        P(("rep", "group", "local"), None),
        P(("rep", "group", "local"), None),
        P(("group", "local"), None, None),
        P(("group", "local"), None, None),
        P(("group", "local"), None, None),
    )
    out_specs = P(("rep", "group", "local"), None)
    return jax.shard_map(shards, mesh=mesh, in_specs=in_specs, out_specs=out_specs, check_vma=False)
```

```python
import functools

import jax
import jax.numpy as jnp
from jax import lax
from jax.experimental import pallas as pl
from jax.experimental.pallas import tpu as pltpu
from jax.sharding import PartitionSpec as P

GROUPS_TOK = 4
VMEM_LIMIT = 16 * 2**20


def expert_rows(rows, gate_mat, up_mat, down_mat):
    gate = jnp.dot(rows, gate_mat, preferred_element_type=jnp.float32)
    up = jnp.dot(rows, up_mat, preferred_element_type=jnp.float32)
    hidden = (jax.nn.silu(gate) * up).astype(jnp.bfloat16)
    return jnp.dot(hidden, down_mat, preferred_element_type=jnp.float32).astype(jnp.bfloat16)


def routed_shards(tokens, gates, expert_ids, w_gate, w_up, w_down):
    tok_rows, width = tokens.shape
    n_group = lax.axis_size("group")
    local_expert_count = lax.axis_size("local")
    capacity = min(tok_rows, tok_rows * GROUPS_TOK // n_group)
    expert_iota = jnp.arange(n_group * local_expert_count, dtype=jnp.int32)
    hits = expert_ids[:, :, None] == expert_iota
    weights = jnp.sum(
        jnp.where(hits, gates.astype(jnp.float32)[:, :, None], jnp.float32(0.0)), axis=1
    )
    member = jnp.any(
        jnp.any(hits, axis=1).reshape(tok_rows, n_group, local_expert_count), axis=2
    ).astype(jnp.int32)
    rank = jnp.cumsum(member, axis=0) - member
    slot_iota = jnp.arange(capacity, dtype=jnp.int32)
    place = (member[:, :, None] == 1) & (rank[:, :, None] == slot_iota)
    place_f = place.astype(jnp.float32)
    outgoing = jnp.einsum(
        "tgc,td->gcd", place.astype(jnp.bfloat16), tokens, preferred_element_type=jnp.float32
    ).astype(jnp.bfloat16)
    slot_weights = jnp.einsum(
        "tgc,tgl->gcl",
        place_f,
        weights.reshape(tok_rows, n_group, local_expert_count),
        precision=lax.Precision.HIGHEST,
    ).astype(jnp.bfloat16)
    send_rows = jnp.broadcast_to(
        outgoing[:, None], (n_group, local_expert_count, capacity, width)
    ).reshape(n_group * local_expert_count, capacity, width)
    send_weights = jnp.transpose(slot_weights, (0, 2, 1)).reshape(
        n_group * local_expert_count, capacity
    )
    received_rows, got_weights = (
        lax.all_to_all(send_rows, ("group", "local"), split_axis=0, concat_axis=0, tiled=True),
        lax.all_to_all(send_weights, ("group", "local"), split_axis=0, concat_axis=0, tiled=True),
    )
    arrived = received_rows.reshape(n_group, local_expert_count, capacity, width)
    own_weights = got_weights.reshape(n_group, local_expert_count, capacity)
    outputs = expert_rows(
        arrived.reshape(n_group * local_expert_count * capacity, width),
        w_gate[0],
        w_up[0],
        w_down[0],
    )
    outputs = outputs.reshape(n_group, local_expert_count, capacity, width)
    masked = jnp.where(own_weights[..., None] > 0, outputs, jnp.zeros_like(outputs))
    returned_rows = lax.all_to_all(
        masked.reshape(n_group * local_expert_count, capacity, width),
        ("group", "local"),
        split_axis=0,
        concat_axis=0,
        tiled=True,
    )
    returned_rows = returned_rows.reshape(n_group, local_expert_count, capacity, width)
    sender_weights = jnp.transpose(slot_weights, (0, 2, 1))
    combined = jnp.einsum(
        "zqa,zqap->zap", sender_weights, returned_rows, preferred_element_type=jnp.float32
    )
    mixed = jnp.einsum("tgc,gcd->td", place_f, combined, precision=lax.Precision.HIGHEST)
    return mixed.astype(jnp.bfloat16)


def over(axis, mask):
    pairs = [(i, i ^ mask) for i in range(4)]
    return lambda v: lax.ppermute(v, axis, pairs)


def expert_kernel(n_pieces, ff_tile, out_tile, me_ref, *refs, loads=()):
    pieces = refs[:n_pieces]
    wg, wu, wd = refs[n_pieces : n_pieces + 3]
    *outs, hidden = refs[n_pieces + 3 :]
    _, ff, width = wd.shape

    table = jnp.concatenate([p[:, pl.ds(width, 128)] for p in pieces], axis=0).astype(jnp.float32)
    lane = lax.broadcasted_iota(jnp.int32, table.shape, 1)
    scale = jnp.sum(jnp.where(lane == me_ref[0], table, 0.0), axis=1, keepdims=True)
    for f in range(ff // ff_tile):
        cols = pl.ds(f * ff_tile, ff_tile)
        for load in loads[2 * f : 2 * f + 2]:
            load.wait()
        x = jnp.concatenate([p[:, pl.ds(0, width)] for p in pieces], axis=0)
        gate = jnp.dot(x, wg[0, :, cols], preferred_element_type=jnp.float32)
        up = jnp.dot(x, wu[0, :, cols], preferred_element_type=jnp.float32)
        hidden[:, cols] = (jax.nn.silu(gate) * up).astype(jnp.bfloat16)
    for load in loads[2 * (ff // ff_tile) :]:
        load.wait()
    for n in range(width // out_tile):
        cols = pl.ds(n * out_tile, out_tile)
        out = jnp.dot(hidden[...], wd[0, :, cols], preferred_element_type=jnp.float32) * scale
        at = 0
        for buf in outs:
            size = buf.shape[0]
            buf[:, cols] = out[at : at + size].astype(buf.dtype)
            at += size


def first_kernel(n_pieces, ff_tile, out_tile, me_ref, *refs):
    weights_hbm = refs[n_pieces : n_pieces + 3]
    weights = refs[n_pieces + 3 : n_pieces + 6]
    load_sems = refs[-1]
    ff = weights[0].shape[2]
    loads, pairs = [], []
    for f in range(ff // ff_tile):
        cols = pl.ds(f * ff_tile, ff_tile)
        pairs += [(w_hbm.at[0, :, cols], w.at[0, :, cols]) for w_hbm, w in zip(weights_hbm[:2], weights[:2])]
    pairs.append((weights_hbm[2], weights[2]))
    for i, (src, dst) in enumerate(pairs):
        loads.append(pltpu.make_async_copy(src, dst, load_sems.at[i]))
        loads[-1].start()
    expert_kernel(
        n_pieces, ff_tile, out_tile, me_ref, *refs[:n_pieces], *weights, *refs[n_pieces + 6 : -1], loads=loads
    )


def experts(pieces, outs, me, weights, first=False):
    n_rows = sum(p.shape[0] for p in pieces)
    _, width, ff = weights[0].shape
    ff_tile, out_tile = ff // 3, width // 5
    vmem = pl.BlockSpec(memory_space=pltpu.VMEM)
    if first:
        weights = [pltpu.with_memory_space_constraint(w, pltpu.HBM) for w in weights]
    return pl.pallas_call(
        functools.partial(first_kernel if first else expert_kernel, len(pieces), ff_tile, out_tile),
        out_shape=[
            *(pltpu.VMEM(w.shape, w.dtype) for w in weights if first),
            *(pltpu.VMEM((rows, width), dtype) for rows, dtype in outs),
        ],
        in_specs=[
            pl.BlockSpec(memory_space=pltpu.SMEM),
            *([vmem] * len(pieces)),
            *([pl.BlockSpec(memory_space=pltpu.HBM) if first else vmem] * 3),
        ],
        out_specs=[vmem] * (len(outs) + 3 * first),
        scratch_shapes=[
            pltpu.VMEM((n_rows, ff), jnp.bfloat16),
            *([pltpu.SemaphoreType.DMA((7,))] if first else []),
        ],
        compiler_params=pltpu.CompilerParams(vmem_limit_bytes=VMEM_LIMIT),
        cost_estimate=pl.CostEstimate(
            flops=6 * n_rows * width * ff,
            bytes_accessed=8 * n_rows * width,
            transcendentals=n_rows * ff,
        ),
    )(me, *pieces, *weights)


def label_kernel(tokens_ref, gates_ref, ids_ref, out_ref, sem):
    width = tokens_ref.shape[1]
    copy = pltpu.make_async_copy(tokens_ref, out_ref.at[:, pl.ds(0, width)], sem)
    copy.start()
    top, rows = gates_ref.shape
    expert = lax.broadcasted_iota(jnp.int32, (128, rows), 0)
    table = jnp.zeros((128, rows), jnp.float32)
    for k in range(top):
        table += jnp.where(ids_ref[k : k + 1] == expert, gates_ref[k : k + 1].astype(jnp.float32), 0.0)
    out_ref[:, pl.ds(width, 128)] = table.T.astype(jnp.bfloat16)
    copy.wait()


def labelled(tokens, gates, expert_ids):
    rows, width = tokens.shape
    return pl.pallas_call(
        label_kernel,
        out_shape=pltpu.VMEM((rows, width + 128), jnp.bfloat16),
        in_specs=[pl.BlockSpec(memory_space=pltpu.HBM)] + [pl.BlockSpec(memory_space=pltpu.VMEM)] * 2,
        out_specs=pl.BlockSpec(memory_space=pltpu.VMEM),
        scratch_shapes=[pltpu.SemaphoreType.DMA],
    )(pltpu.with_memory_space_constraint(tokens, pltpu.HBM), gates.T, expert_ids.T)


def after(value, *done):
    return lax.optimization_barrier((value, *done))[0]


def gathered_shards(tokens, gates, expert_ids, w_gate, w_up, w_down):
    block = tokens.shape[0]
    X, Y = over("local", 1), over("local", 2)
    Z1, Z2 = over("group", 1), over("group", 2)
    me = lax.axis_index("group") * 4 + lax.axis_index("local")

    own = labelled(tokens, gates, expert_ids)

    half = block // 2
    f32, bf16 = jnp.float32, jnp.bfloat16
    me = me.astype(jnp.int32).reshape(1)

    e1, own_x, own_y, e2 = Z1(own), X(own), Y(own), Z2(own)
    own_a = Y(own_x[:half])
    own_b = X(own_y[half:])
    *weights, k0, k0_x, k0_y = experts(
        (own, own_x, own_y), ((block, f32),) * 3, me, (w_gate, w_up, w_down), first=True
    )
    e2 = after(e2, own_a, own_b, e1, k0_x)
    e2_x = X(e2)
    e2_y = Y(e2)
    e3 = Z1(e2)
    e2_a = Y(e2_x[:half])
    e2_b = X(e2_y[half:])
    e3 = after(e3, e2_x, e2_y)
    e3_x = X(e3)
    e3_y = Y(e3)
    e1_yx = Z1(after(jnp.concatenate([own_y, own_x]), e3))
    e1_d = Z1(after(jnp.concatenate([own_a, own_b]), e3))
    k2, k2_l, send_2, k0_d = experts(
        (e2, e2_y, e2_x, e2_a, e2_b, own_a, own_b),
        ((block, f32), (block, f32), (2 * block, bf16), (block, f32)),
        me,
        weights,
    )
    got_2 = X(send_2)
    e3_a = Y(after(e3_x, e3_y, k2)[:half])
    e3_b = X(after(e3_y, e3_x, k2)[half:])
    k3, k3_x, k3_y, send_a, send_b = experts(
        (after(e3, e1_yx), e3_x, e3_y, e3_a, e3_b),
        (*(((block, f32),) * 3), (half, bf16), (half, bf16)),
        me,
        weights,
    )

    def for_x(part, got):
        return jnp.concatenate([part[:half] + got.astype(f32), part[half:]]).astype(bf16)

    def for_y(part, got):
        return jnp.concatenate([part[:half], part[half:] + got.astype(f32)]).astype(bf16)

    got_a = Y(send_a)
    got_b = X(send_b)
    k1, send_1, to_own = experts(
        (after(e1, send_a), e1_yx, e1_d),
        ((block, f32), (block, bf16), (2 * block, bf16)),
        me,
        weights,
    )
    got_x = X(after(for_x(k3_x, got_a), got_b, k1))
    got_y = Y(after(for_y(k3_y, got_b), got_a, k1))
    r3 = (k3 + got_x.astype(f32) + got_y.astype(f32)).astype(bf16)
    last_2 = Y((k2_l + got_2[block:].astype(f32)).astype(bf16))
    r2 = k2 + got_2[:block].astype(f32) + last_2.astype(f32)
    from_1 = Z1(to_own)
    got_1 = Y(after(send_1, got_x, got_y))
    r1 = (k1 + got_1.astype(f32)).astype(bf16)
    got_3 = Z1(r3)
    from_far = Z2((r2 + got_3.astype(f32)).astype(bf16))
    near = Z1(after(r1, got_3))
    k0_x = k0_x + from_1[:block].astype(f32)
    k0_d = (k0_d + from_1[block:].astype(f32)).astype(bf16)
    n_a = Y(after(k0_d, got_x, got_y)[:half])
    n_b = X(after(k0_d, got_x, got_y)[half:])
    n_x = X(for_x(k0_x, n_a))
    n_y = Y(for_y(k0_y, n_b))
    r0 = k0 + n_x.astype(f32) + n_y.astype(f32)
    return (r0 + near.astype(f32) + from_far.astype(f32)).astype(bf16)


def shards(tokens, *rest):
    tok_rows = tokens.shape[0]
    n_group, n_local = lax.axis_size("group"), lax.axis_size("local")
    capacity = min(tok_rows, tok_rows * GROUPS_TOK // n_group)
    if capacity == tok_rows and n_group == 4 and n_local == 4:
        return gathered_shards(tokens, *rest)
    return routed_shards(tokens, *rest)


def solution(mesh):
    in_specs = (
        P(("rep", "group", "local"), None),
        P(("rep", "group", "local"), None),
        P(("rep", "group", "local"), None),
        P(("group", "local"), None, None),
        P(("group", "local"), None, None),
        P(("group", "local"), None, None),
    )
    out_specs = P(("rep", "group", "local"), None)
    return jax.shard_map(shards, mesh=mesh, in_specs=in_specs, out_specs=out_specs, check_vma=False)
```

```python
import functools

import jax
import jax.numpy as jnp
from jax import lax
from jax.experimental import pallas as pl
from jax.experimental.pallas import tpu as pltpu
from jax.sharding import PartitionSpec as P

GROUPS_TOK = 4
VMEM_LIMIT = 16 * 2**20


def expert_rows(rows, gate_mat, up_mat, down_mat):
    gate = jnp.dot(rows, gate_mat, preferred_element_type=jnp.float32)
    up = jnp.dot(rows, up_mat, preferred_element_type=jnp.float32)
    hidden = (jax.nn.silu(gate) * up).astype(jnp.bfloat16)
    return jnp.dot(hidden, down_mat, preferred_element_type=jnp.float32).astype(jnp.bfloat16)


def routed_shards(tokens, gates, expert_ids, w_gate, w_up, w_down):
    tok_rows, width = tokens.shape
    n_group = lax.axis_size("group")
    local_expert_count = lax.axis_size("local")
    capacity = min(tok_rows, tok_rows * GROUPS_TOK // n_group)
    expert_iota = jnp.arange(n_group * local_expert_count, dtype=jnp.int32)
    hits = expert_ids[:, :, None] == expert_iota
    weights = jnp.sum(
        jnp.where(hits, gates.astype(jnp.float32)[:, :, None], jnp.float32(0.0)), axis=1
    )
    member = jnp.any(
        jnp.any(hits, axis=1).reshape(tok_rows, n_group, local_expert_count), axis=2
    ).astype(jnp.int32)
    rank = jnp.cumsum(member, axis=0) - member
    slot_iota = jnp.arange(capacity, dtype=jnp.int32)
    place = (member[:, :, None] == 1) & (rank[:, :, None] == slot_iota)
    place_f = place.astype(jnp.float32)
    outgoing = jnp.einsum(
        "tgc,td->gcd", place.astype(jnp.bfloat16), tokens, preferred_element_type=jnp.float32
    ).astype(jnp.bfloat16)
    slot_weights = jnp.einsum(
        "tgc,tgl->gcl",
        place_f,
        weights.reshape(tok_rows, n_group, local_expert_count),
        precision=lax.Precision.HIGHEST,
    ).astype(jnp.bfloat16)
    send_rows = jnp.broadcast_to(
        outgoing[:, None], (n_group, local_expert_count, capacity, width)
    ).reshape(n_group * local_expert_count, capacity, width)
    send_weights = jnp.transpose(slot_weights, (0, 2, 1)).reshape(
        n_group * local_expert_count, capacity
    )
    received_rows, got_weights = (
        lax.all_to_all(send_rows, ("group", "local"), split_axis=0, concat_axis=0, tiled=True),
        lax.all_to_all(send_weights, ("group", "local"), split_axis=0, concat_axis=0, tiled=True),
    )
    arrived = received_rows.reshape(n_group, local_expert_count, capacity, width)
    own_weights = got_weights.reshape(n_group, local_expert_count, capacity)
    outputs = expert_rows(
        arrived.reshape(n_group * local_expert_count * capacity, width),
        w_gate[0],
        w_up[0],
        w_down[0],
    )
    outputs = outputs.reshape(n_group, local_expert_count, capacity, width)
    masked = jnp.where(own_weights[..., None] > 0, outputs, jnp.zeros_like(outputs))
    returned_rows = lax.all_to_all(
        masked.reshape(n_group * local_expert_count, capacity, width),
        ("group", "local"),
        split_axis=0,
        concat_axis=0,
        tiled=True,
    )
    returned_rows = returned_rows.reshape(n_group, local_expert_count, capacity, width)
    sender_weights = jnp.transpose(slot_weights, (0, 2, 1))
    combined = jnp.einsum(
        "zqa,zqap->zap", sender_weights, returned_rows, preferred_element_type=jnp.float32
    )
    mixed = jnp.einsum("tgc,gcd->td", place_f, combined, precision=lax.Precision.HIGHEST)
    return mixed.astype(jnp.bfloat16)


def over(axis, mask):
    pairs = [(i, i ^ mask) for i in range(4)]
    return lambda v: lax.ppermute(v, axis, pairs)


def expert_kernel(n_pieces, ff_tile, out_tile, me_ref, *refs, loads=()):
    pieces = refs[:n_pieces]
    wg, wu, wd = refs[n_pieces : n_pieces + 3]
    *outs, hidden = refs[n_pieces + 3 :]
    _, ff, width = wd.shape

    table = jnp.concatenate([p[:, pl.ds(width, 128)] for p in pieces], axis=0).astype(jnp.float32)
    lane = lax.broadcasted_iota(jnp.int32, table.shape, 1)
    scale = jnp.sum(jnp.where(lane == me_ref[0], table, 0.0), axis=1, keepdims=True)
    for f in range(ff // ff_tile):
        cols = pl.ds(f * ff_tile, ff_tile)
        for load in loads[2 * f : 2 * f + 2]:
            load.wait()
        x = jnp.concatenate([p[:, pl.ds(0, width)] for p in pieces], axis=0)
        gate = jnp.dot(x, wg[0, :, cols], preferred_element_type=jnp.float32)
        up = jnp.dot(x, wu[0, :, cols], preferred_element_type=jnp.float32)
        hidden[:, cols] = (jax.nn.silu(gate) * up).astype(jnp.bfloat16)
    for load in loads[2 * (ff // ff_tile) :]:
        load.wait()
    for n in range(width // out_tile):
        cols = pl.ds(n * out_tile, out_tile)
        out = jnp.dot(hidden[...], wd[0, :, cols], preferred_element_type=jnp.float32) * scale
        at = 0
        for buf in outs:
            size = buf.shape[0]
            buf[:, cols] = out[at : at + size].astype(buf.dtype)
            at += size


def first_kernel(n_pieces, ff_tile, out_tile, me_ref, *refs):
    weights_hbm = refs[n_pieces : n_pieces + 3]
    weights = refs[n_pieces + 3 : n_pieces + 6]
    load_sems = refs[-1]
    ff = weights[0].shape[2]
    loads, pairs = [], []
    for f in range(ff // ff_tile):
        cols = pl.ds(f * ff_tile, ff_tile)
        pairs += [(w_hbm.at[0, :, cols], w.at[0, :, cols]) for w_hbm, w in zip(weights_hbm[:2], weights[:2])]
    pairs.append((weights_hbm[2], weights[2]))
    for i, (src, dst) in enumerate(pairs):
        loads.append(pltpu.make_async_copy(src, dst, load_sems.at[i]))
        loads[-1].start()
    expert_kernel(
        n_pieces, ff_tile, out_tile, me_ref, *refs[:n_pieces], *weights, *refs[n_pieces + 6 : -1], loads=loads
    )


def experts(pieces, outs, me, weights, first=False):
    n_rows = sum(p.shape[0] for p in pieces)
    _, width, ff = weights[0].shape
    ff_tile, out_tile = ff // 3, width // 2
    vmem = pl.BlockSpec(memory_space=pltpu.VMEM)
    if first:
        weights = [pltpu.with_memory_space_constraint(w, pltpu.HBM) for w in weights]
    return pl.pallas_call(
        functools.partial(first_kernel if first else expert_kernel, len(pieces), ff_tile, out_tile),
        out_shape=[
            *(pltpu.VMEM(w.shape, w.dtype) for w in weights if first),
            *(pltpu.VMEM((rows, width), dtype) for rows, dtype in outs),
        ],
        in_specs=[
            pl.BlockSpec(memory_space=pltpu.SMEM),
            *([vmem] * len(pieces)),
            *([pl.BlockSpec(memory_space=pltpu.HBM) if first else vmem] * 3),
        ],
        out_specs=[vmem] * (len(outs) + 3 * first),
        scratch_shapes=[
            pltpu.VMEM((n_rows, ff), jnp.bfloat16),
            *([pltpu.SemaphoreType.DMA((7,))] if first else []),
        ],
        compiler_params=pltpu.CompilerParams(vmem_limit_bytes=VMEM_LIMIT),
        cost_estimate=pl.CostEstimate(
            flops=6 * n_rows * width * ff,
            bytes_accessed=8 * n_rows * width,
            transcendentals=n_rows * ff,
        ),
    )(me, *pieces, *weights)


def label_kernel(tokens_ref, gates_ref, ids_ref, out_ref, sem):
    width = tokens_ref.shape[1]
    copy = pltpu.make_async_copy(tokens_ref, out_ref.at[:, pl.ds(0, width)], sem)
    copy.start()
    top, rows = gates_ref.shape
    expert = lax.broadcasted_iota(jnp.int32, (128, rows), 0)
    table = jnp.zeros((128, rows), jnp.float32)
    for k in range(top):
        table += jnp.where(ids_ref[k : k + 1] == expert, gates_ref[k : k + 1].astype(jnp.float32), 0.0)
    out_ref[:, pl.ds(width, 128)] = table.T.astype(jnp.bfloat16)
    copy.wait()


def labelled(tokens, gates, expert_ids):
    rows, width = tokens.shape
    return pl.pallas_call(
        label_kernel,
        out_shape=pltpu.VMEM((rows, width + 128), jnp.bfloat16),
        in_specs=[pl.BlockSpec(memory_space=pltpu.HBM)] + [pl.BlockSpec(memory_space=pltpu.VMEM)] * 2,
        out_specs=pl.BlockSpec(memory_space=pltpu.VMEM),
        scratch_shapes=[pltpu.SemaphoreType.DMA],
    )(pltpu.with_memory_space_constraint(tokens, pltpu.HBM), gates.T, expert_ids.T)


def after(value, *done):
    return lax.optimization_barrier((value, *done))[0]


def gathered_shards(tokens, gates, expert_ids, w_gate, w_up, w_down):
    block = tokens.shape[0]
    X, Y = over("local", 1), over("local", 2)
    Z1, Z2 = over("group", 1), over("group", 2)
    me = lax.axis_index("group") * 4 + lax.axis_index("local")

    own = labelled(tokens, gates, expert_ids)

    half = block // 2
    f32, bf16 = jnp.float32, jnp.bfloat16
    me = me.astype(jnp.int32).reshape(1)

    e1, own_x, own_y, e2 = Z1(own), X(own), Y(own), Z2(own)
    own_a = Y(own_x[:half])
    own_b = X(own_y[half:])
    *weights, k0, k0_x, k0_y = experts(
        (own, own_x, own_y), ((block, f32),) * 3, me, (w_gate, w_up, w_down), first=True
    )
    e2 = after(e2, own_a, own_b, e1, k0_x)
    e2_x = X(e2)
    e2_y = Y(e2)
    e3 = Z1(e2)
    e2_a = Y(e2_x[:half])
    e2_b = X(e2_y[half:])
    e3 = after(e3, e2_x, e2_y)
    e3_x = X(e3)
    e3_y = Y(e3)
    e1_yx = Z1(after(jnp.concatenate([own_y, own_x]), e3))
    e1_d = Z1(after(jnp.concatenate([own_a, own_b]), e3))
    k2, k2_l, send_2, k0_d = experts(
        (e2, e2_y, e2_x, e2_a, e2_b, own_a, own_b),
        ((block, f32), (block, f32), (2 * block, bf16), (block, f32)),
        me,
        weights,
    )
    got_2 = X(send_2)
    e3_a = Y(after(e3_x, e3_y, k2)[:half])
    e3_b = X(after(e3_y, e3_x, k2)[half:])
    k3, k3_x, k3_y, send_a, send_b = experts(
        (after(e3, e1_yx), e3_x, e3_y, e3_a, e3_b),
        (*(((block, f32),) * 3), (half, bf16), (half, bf16)),
        me,
        weights,
    )

    def for_x(part, got):
        return jnp.concatenate([part[:half] + got.astype(f32), part[half:]]).astype(bf16)

    def for_y(part, got):
        return jnp.concatenate([part[:half], part[half:] + got.astype(f32)]).astype(bf16)

    got_a = Y(send_a)
    got_b = X(send_b)
    k1, send_1, to_own = experts(
        (after(e1, send_a), e1_yx, e1_d),
        ((block, f32), (block, bf16), (2 * block, bf16)),
        me,
        weights,
    )
    got_x = X(after(for_x(k3_x, got_a), got_b, k1))
    got_y = Y(after(for_y(k3_y, got_b), got_a, k1))
    r3 = (k3 + got_x.astype(f32) + got_y.astype(f32)).astype(bf16)
    last_2 = Y((k2_l + got_2[block:].astype(f32)).astype(bf16))
    r2 = k2 + got_2[:block].astype(f32) + last_2.astype(f32)
    from_1 = Z1(to_own)
    got_1 = Y(after(send_1, got_x, got_y))
    r1 = (k1 + got_1.astype(f32)).astype(bf16)
    got_3 = Z1(r3)
    from_far = Z2((r2 + got_3.astype(f32)).astype(bf16))
    near = Z1(after(r1, got_3))
    k0_x = k0_x + from_1[:block].astype(f32)
    k0_d = (k0_d + from_1[block:].astype(f32)).astype(bf16)
    n_a = Y(after(k0_d, got_x, got_y)[:half])
    n_b = X(after(k0_d, got_x, got_y)[half:])
    n_x = X(for_x(k0_x, n_a))
    n_y = Y(for_y(k0_y, n_b))
    r0 = k0 + n_x.astype(f32) + n_y.astype(f32)
    return (r0 + near.astype(f32) + from_far.astype(f32)).astype(bf16)


def shards(tokens, *rest):
    tok_rows = tokens.shape[0]
    n_group, n_local = lax.axis_size("group"), lax.axis_size("local")
    capacity = min(tok_rows, tok_rows * GROUPS_TOK // n_group)
    if capacity == tok_rows and n_group == 4 and n_local == 4:
        return gathered_shards(tokens, *rest)
    return routed_shards(tokens, *rest)


def solution(mesh):
    in_specs = (
        P(("rep", "group", "local"), None),
        P(("rep", "group", "local"), None),
        P(("rep", "group", "local"), None),
        P(("group", "local"), None, None),
        P(("group", "local"), None, None),
        P(("group", "local"), None, None),
    )
    out_specs = P(("rep", "group", "local"), None)
    return jax.shard_map(shards, mesh=mesh, in_specs=in_specs, out_specs=out_specs, check_vma=False)
```
